32 devices in a mesh: member: 2 (over y), lat: 4 (over z), lev: 2 (over x), fld: 2 (over core).
Axes of the slice: x: 2, y: 2, z: 4, core: 2. Of those that a mesh axis runs over, the one named last changes fastest.
Arguments:
- grid_state: bfloat16 [4, 48, 480, 1920], P(('member', 'fld'), 'lev', 'lat'), parts along dimension 0, may hold values from -6 to 6
- lat_order: int32 [480], replicated, may hold values from 0 to 479, each once
- slot_wave: int32 [384], replicated, may hold values from 0 to 383, each once
- truncation: int32 [384], replicated, may hold values from 288 to 383, as said below
- zonal_wind: float32 [480], replicated, may hold values from -3 to 3
- zonal_rate: float32 [480], replicated, may hold values from 0.0003 to 0.003
- quad_weight: float32 [480], replicated, may hold values from 0.02 to 0.09
- legendre: bfloat16 [384, 384, 480], P(('lat', 'lev')), may hold values from -5 to 5
- vert_modes: float32 [48, 48], replicated, may hold values from -0.875 to 0.875
- vert_project: float32 [48, 48], replicated, may hold values from -0.875 to 0.875
- mode_rates: float32 [48], replicated, may hold values from 0.5 to 8
- thermal_into_spread_matrix: float32 [48, 48], replicated, may hold values from -0.875 to 0.875
- pressure_balance_matrix: float32 [48, 48], replicated, may hold values from -0.875 to 0.875
Outputs:
- grid_new: bfloat16 [4, 48, 480, 1920], P(('member', 'fld'), 'lev', 'lat'), parts along dimension 0
The draws below stay inside these ranges and needn't reach their ends.
There are 2 independent parts, one for each index of `member`. The reference program is written for one: setup_inputs(seed, part) draws one part's arguments, and reference() takes and returns one part's arrays. A program takes and returns all parts, laid end to end along the dimension named above; an argument that names none is the same for every part. Nothing has to cross between parts.
Inputs may be any that keep to these rules, and one draw needn't show every extreme that they name: `lat_order`: each latitude once. `slot_wave`: each wavenumber once. truncation[m] is never below m, and truncation[383] = 383.
All inputs are finite; a program needn't handle non-finite values.
Results may differ from the reference program's by a relative error of at most 0.0071.
Values may be sent and summed in bfloat16 or wider, within the bound.
A program may use at most 128 MiB of HBM per device.

```python
import math
import jax
import jax.numpy as jnp
from jax import lax

COUPLED_UNKNOWNS = 2
HEIGHT_LAYERS = 48
NLAT = 480
NLON = 1920
EAST_MODES = 384


def draw_truncation(key, part):
    wavenums = jnp.arange(EAST_MODES, dtype=jnp.int32)
    spare = EAST_MODES - 1 - wavenums
    cutoff = jax.random.randint(key, (EAST_MODES,), 0, spare // 4 + 1)
    return (EAST_MODES - 1 - cutoff).astype(jnp.int32)


def level_of(key, shape, cuts, low, top_value):
    factor_of = 1.0
    for dim, parts in cuts:
        steps = jax.random.uniform(jax.random.fold_in(jax.random.fold_in(key, 6), dim), (parts,), jnp.float32, low / len(cuts), top_value / len(cuts))
        factor_of = factor_of * jnp.repeat(jnp.exp(steps), shape[dim] // parts).reshape((-1,) + (1,) * (len(shape) - 1 - dim))
    return factor_of


def noise(stream_key, shape, width, reach, cuts=(), kind=jnp.bfloat16):
    gain = level_of(stream_key, shape, cuts, -0.22, 0.18) if cuts else 1.0
    result = jax.random.normal(stream_key, shape, jnp.float32) * width * gain
    return jnp.minimum(jnp.maximum(result, -reach), reach).astype(kind)


def setup_inputs(seed: int = 0, part: int = 0) -> dict:
    streams_of = jax.random.split(jax.random.key(seed), 14)
    part_splits = jax.random.split(jax.random.fold_in(streams_of[13], part), 14)
    grid_state = noise(part_splits[0], (COUPLED_UNKNOWNS, HEIGHT_LAYERS, NLAT, NLON), 1.0, 6.0, ((0, 2), (1, 2), (2, 4)))
    lat_order = jax.random.permutation(streams_of[1], NLAT).astype(jnp.int32)
    slot_wave = jax.random.permutation(streams_of[2], EAST_MODES).astype(jnp.int32)
    truncation = draw_truncation(jax.random.fold_in(streams_of[13], 71), part)
    zonal_wind = noise(streams_of[4], (NLAT,), 0.5, 3.0, (), jnp.float32)
    zonal_rate = jnp.clip(jnp.exp(jax.random.uniform(streams_of[5], (NLAT,), jnp.float32, math.log(0.0003), math.log(0.003))), 0.0003, 0.003)
    quad_weight = jnp.clip(jnp.exp(jax.random.uniform(streams_of[6], (NLAT,), jnp.float32, math.log(0.02), math.log(0.09))), 0.02, 0.09)
    legendre = noise(streams_of[7], (EAST_MODES, EAST_MODES, NLAT), 1.0, 5.0, ((0, 8),))
    vert_modes = noise(streams_of[8], (HEIGHT_LAYERS, HEIGHT_LAYERS), HEIGHT_LAYERS ** -0.5, 0.875, (), jnp.float32)
    vert_project = noise(streams_of[9], (HEIGHT_LAYERS, HEIGHT_LAYERS), HEIGHT_LAYERS ** -0.5, 0.875, (), jnp.float32)
    mode_rates = jnp.clip(jnp.exp(jax.random.uniform(streams_of[10], (HEIGHT_LAYERS,), jnp.float32, math.log(0.5), math.log(8.0))), 0.5, 8.0)
    thermal_into_spread_matrix = noise(streams_of[11], (HEIGHT_LAYERS, HEIGHT_LAYERS), HEIGHT_LAYERS ** -0.5, 0.875, (), jnp.float32)
    pressure_balance_matrix = noise(streams_of[12], (HEIGHT_LAYERS, HEIGHT_LAYERS), HEIGHT_LAYERS ** -0.5, 0.875, (), jnp.float32)
    return dict(grid_state=grid_state, lat_order=lat_order, slot_wave=slot_wave, truncation=truncation, zonal_wind=zonal_wind, zonal_rate=zonal_rate, quad_weight=quad_weight, legendre=legendre, vert_modes=vert_modes, vert_project=vert_project, mode_rates=mode_rates, thermal_into_spread_matrix=thermal_into_spread_matrix, pressure_balance_matrix=pressure_balance_matrix)


PRECISE = lax.Precision.HIGHEST


def dft_table(wavenums):
    columns = jnp.arange(NLON, dtype=jnp.int32)
    turns = (columns[:, None] * wavenums[None, :]) % NLON
    angles = turns.astype(jnp.float32) * (2.0 * jnp.pi / NLON)
    return jnp.stack([jnp.cos(angles), -jnp.sin(angles)], axis=1).astype(jnp.bfloat16)


def layer_eigen_basis(matrix, columns):
    return jnp.einsum("skcj,ij->skci", columns, matrix, precision=PRECISE)


def analyse_slot(pieces):
    return jnp.dot(pieces[0], pieces[1], preferred_element_type=jnp.float32)


def synth_slot(pieces):
    return lax.dot_general(pieces[0], pieces[1], (((0,), (0,)), ((), ())), preferred_element_type=jnp.float32)


def reference(grid_state, lat_order, slot_wave, truncation, zonal_wind, zonal_rate, quad_weight, legendre, vert_modes, vert_project, mode_rates, thermal_into_spread_matrix, pressure_balance_matrix):
    table = dft_table(slot_wave.astype(jnp.int32)).reshape(NLON, 2 * EAST_MODES)
    winds = zonal_wind[lat_order]
    rates = zonal_rate[lat_order]
    weights = quad_weight[lat_order]
    values = grid_state.astype(jnp.float32)
    flux = (values * (winds[None, None, :, None] + values)).astype(jnp.bfloat16)
    count_rows = COUPLED_UNKNOWNS * HEIGHT_LAYERS * NLAT
    plain = jnp.dot(grid_state.reshape(count_rows, NLON), table, preferred_element_type=jnp.float32) * NLON ** -0.5
    moved = jnp.dot(flux.reshape(count_rows, NLON), table, preferred_element_type=jnp.float32) * NLON ** -0.5
    plain = plain.reshape(COUPLED_UNKNOWNS, HEIGHT_LAYERS, NLAT, 2, EAST_MODES)
    moved = moved.reshape(COUPLED_UNKNOWNS, HEIGHT_LAYERS, NLAT, 2, EAST_MODES)
    wave_float = slot_wave.astype(jnp.float32)
    factor = rates[:, None] * wave_float[None, :]
    real_part = (plain[:, :, :, 0] + factor * moved[:, :, :, 1]) * weights[:, None]
    imag_part = (plain[:, :, :, 1] - factor * moved[:, :, :, 0]) * weights[:, None]
    fourier = jnp.stack([real_part, imag_part], axis=3).astype(jnp.bfloat16)
    position = jnp.zeros((NLAT,), jnp.int32).at[lat_order].set(jnp.arange(NLAT, dtype=jnp.int32))
    fourier = jnp.take(fourier, position, axis=2)
    gathered = jnp.transpose(fourier, (4, 2, 0, 3, 1)).reshape(EAST_MODES, NLAT, COUPLED_UNKNOWNS * 2 * HEIGHT_LAYERS)
    harmonic_current = lax.map(analyse_slot, (legendre, gathered))
    limits = truncation[slot_wave]
    counts = limits - slot_wave + 1
    degree = jnp.arange(EAST_MODES, dtype=jnp.int32)
    valid = degree[None, :] < counts[:, None]
    harmonic_current = jnp.where(valid[:, :, None], harmonic_current, jnp.float32(0.0))
    harmonic_current = harmonic_current.reshape(EAST_MODES, EAST_MODES, COUPLED_UNKNOWNS, 2, HEIGHT_LAYERS)
    outflow_rate_coeffs = harmonic_current[:, :, 0]
    thermal_coeffs = harmonic_current[:, :, 1]
    n_deg = (slot_wave[:, None] + degree[None, :]).astype(jnp.float32)
    elliptic_inverse_scale = (n_deg * (n_deg + 1.0) / (EAST_MODES * (EAST_MODES - 1)))[:, :, None, None]
    outflow_rate_source = outflow_rate_coeffs + elliptic_inverse_scale * layer_eigen_basis(thermal_into_spread_matrix, thermal_coeffs)
    projected = layer_eigen_basis(vert_project, outflow_rate_source) / (1.0 + elliptic_inverse_scale * mode_rates)
    outflow_rate_next = layer_eigen_basis(vert_modes, projected)
    thermal_next = thermal_coeffs - layer_eigen_basis(pressure_balance_matrix, outflow_rate_next)
    harmonic_next = jnp.stack([outflow_rate_next, thermal_next], axis=2).astype(jnp.bfloat16).reshape(EAST_MODES, EAST_MODES, COUPLED_UNKNOWNS * 2 * HEIGHT_LAYERS)
    back = lax.map(synth_slot, (legendre, harmonic_next)) * EAST_MODES ** -0.5
    back = jnp.take(back, lat_order, axis=1).astype(jnp.bfloat16)
    back = back.reshape(EAST_MODES, NLAT, COUPLED_UNKNOWNS, 2, HEIGHT_LAYERS)
    leading = jnp.transpose(back, (3, 0, 2, 4, 1)).reshape(2 * EAST_MODES, count_rows)
    grid_out = lax.dot_general(leading, table, (((0,), (1,)), ((), ())), preferred_element_type=jnp.float32) * EAST_MODES ** -0.5
    return grid_out.reshape(COUPLED_UNKNOWNS, HEIGHT_LAYERS, NLAT, NLON).astype(jnp.bfloat16)
```

```python
import jax
import jax.numpy as jnp
from jax import lax
from jax.sharding import PartitionSpec as P

PRECISE = lax.Precision.HIGHEST
CHUNKS = 1


def wave_table(waves, nlon):
    step = next(d for d in range(int(nlon**0.5), 0, -1) if nlon % d == 0)
    unit = 2.0 * jnp.pi / nlon
    low = (waves[:, None] * jnp.arange(step, dtype=jnp.int32)[None, :]) % nlon
    high = (waves[:, None] * (step * jnp.arange(nlon // step, dtype=jnp.int32))[None, :]) % nlon
    low = low.astype(jnp.float32) * unit
    high = high.astype(jnp.float32) * unit
    cl, sl = jnp.cos(low)[:, None, :], jnp.sin(low)[:, None, :]
    ch, sh = jnp.cos(high)[:, :, None], jnp.sin(high)[:, :, None]
    cosine = (ch * cl - sh * sl).reshape(-1, nlon)
    sine = (sh * cl + ch * sl).reshape(-1, nlon)
    return jnp.stack([cosine, -sine], axis=0).astype(jnp.bfloat16)


def local(
    grid_state,
    lat_order,
    slot_wave,
    truncation,
    zonal_wind,
    zonal_rate,
    quad_weight,
    legendre,
    vert_modes,
    vert_project,
    mode_rates,
    thermal_into_spread_matrix,
    pressure_balance_matrix,
):
    levd, latd, nlon = grid_state.shape[1:]
    slots = legendre.shape[0]
    nmodes = slot_wave.shape[0]
    nlat = lat_order.shape[0]
    nlev = vert_modes.shape[0]
    nlats = lax.axis_size("lat")
    nlevs = lax.axis_size("lev")
    nfld = lax.axis_size("fld")
    lat_index = lax.axis_index("lat")
    lev_index = lax.axis_index("lev")
    fld_index = lax.axis_index("fld")
    owners = nlats * nlevs
    dests = owners * nfld
    per = -(-slots // nfld)
    spare = per * nfld - slots
    chunks = CHUNKS if per % CHUNKS == 0 else 1
    part = per // chunks

    waves = jnp.pad(slot_wave.reshape(owners, slots), ((0, 0), (0, spare)))
    waves = waves.reshape(dests, per)
    me = (lat_index * nlevs + lev_index) * nfld + fld_index
    my_waves = lax.dynamic_index_in_dim(waves, me, 0, keepdims=False)
    leg = jnp.pad(legendre, ((0, spare), (0, 0), (0, 0)))
    leg = lax.dynamic_slice_in_dim(leg, fld_index * per, per, 0)
    lats = jnp.arange(nlat, dtype=jnp.int32)
    hits = lat_order[:, None] == lats[None, :]
    leg = jnp.einsum(
        "skl,rl->skr", leg, hits.astype(jnp.bfloat16), preferred_element_type=jnp.float32
    ).astype(jnp.bfloat16)

    my_hits = lax.dynamic_slice_in_dim(hits, lat_index * latd, latd, 0)
    pick = lambda column: jnp.sum(jnp.where(my_hits, column[None, :], 0.0), axis=1)
    wind, rate, weight = pick(zonal_wind), pick(zonal_rate), pick(quad_weight)
    grid = grid_state[0]
    values = grid.astype(jnp.float32)
    flux = (values * (wind[None, :, None] + values)).astype(jnp.bfloat16)

    degree = jnp.arange(nmodes, dtype=jnp.int32)
    mode_hits = my_waves[:, None] == degree[None, :]
    limits = jnp.sum(jnp.where(mode_hits, truncation[None, :], 0), axis=1)
    n_int = my_waves[:, None] + degree[None, :]
    valid = n_int <= limits[:, None]
    n_deg = n_int.astype(jnp.float32)
    h = n_deg * (n_deg + 1.0) / (nmodes * (nmodes - 1))

    mixed = jnp.dot(vert_project, thermal_into_spread_matrix, precision=PRECISE)
    into = jnp.concatenate([vert_project, mixed], axis=1)
    pressed = jnp.dot(pressure_balance_matrix, vert_modes, precision=PRECISE)
    out_of = jnp.concatenate([vert_modes, -pressed], axis=0)

    returned, tables = [], []
    for i in range(chunks):
        cut = slice(i * part, (i + 1) * part)
        w = waves[:, cut]
        table = wave_table(w.reshape(-1), nlon).reshape(2, dests, part, nlon)
        table = jnp.transpose(table, (1, 0, 2, 3))
        dims = (((3,), (2,)), ((), ()))
        scale = nlon ** (-0.5)
        plain = lax.dot_general(table, grid, dims, preferred_element_type=jnp.float32) * scale
        moved = lax.dot_general(table, flux, dims, preferred_element_type=jnp.float32) * scale
        factor = w.astype(jnp.float32)[:, :, None, None] * rate
        real = (plain[:, 0] + factor * moved[:, 1]) * weight
        imag = (plain[:, 1] - factor * moved[:, 0]) * weight
        fourier = jnp.stack([real, imag], axis=1).astype(jnp.bfloat16)
        arrived = lax.all_to_all(
            fourier, ("lat", "lev", "fld"), split_axis=0, concat_axis=0, tiled=True
        )
        arrived = arrived.reshape(nlats, nlevs, nfld, 2, part, levd, latd)
        arranged = jnp.transpose(arrived, (4, 3, 2, 1, 5, 0, 6)).reshape(part, 4 * nlev, nlat)
        mine = leg[cut]
        spec = jnp.einsum("sxr,skr->sxk", arranged, mine, preferred_element_type=jnp.float32)
        spec = spec.reshape(part, 2, 2, nlev, nmodes)
        hc = h[cut][:, None, None, :]
        vc = valid[cut][:, None, None, :]
        div = jnp.where(vc, spec[:, :, 0], 0.0)
        temp = jnp.where(vc, spec[:, :, 1], 0.0)
        source = jnp.concatenate([div, hc * temp], axis=2)
        projected = jnp.einsum("ij,scjk->scik", into, source, precision=lax.Precision.HIGH)
        projected = projected / (1.0 + hc * mode_rates[:, None])
        new = jnp.einsum("ij,scjk->scik", out_of, projected, precision=lax.Precision.HIGH)
        new = new.reshape(part, 2, 2, nlev, nmodes)
        new = jnp.stack([new[:, :, 0], temp + new[:, :, 1]], axis=2).astype(jnp.bfloat16)
        new = new.reshape(part, 4 * nlev, nmodes)
        back = jnp.einsum("sxk,skr->sxr", new, mine, preferred_element_type=jnp.float32)
        back = (back * nmodes ** (-0.5)).astype(jnp.bfloat16)
        back = back.reshape(part, 2, nfld, nlevs, levd, nlats, latd)
        outgoing = jnp.transpose(back, (5, 3, 2, 1, 0, 4, 6)).reshape(dests, 2, part, levd, latd)
        returned.append(
            lax.all_to_all(
                outgoing, ("lat", "lev", "fld"), split_axis=0, concat_axis=0, tiled=True
            )
        )
        tables.append(table)
    leading = jnp.stack(returned, axis=0)
    table = jnp.stack(tables, axis=0)
    dims = (((0, 1, 2, 3), (0, 1, 2, 3)), ((), ()))
    grid_out = lax.dot_general(leading, table, dims, preferred_element_type=jnp.float32)
    return (grid_out * nmodes ** (-0.5)).astype(jnp.bfloat16)[None]


def solution(mesh):
    in_specs = (
        P(("member", "fld"), "lev", "lat", None),
        P(),
        P(),
        P(),
        P(),
        P(),
        P(),
        P(("lat", "lev"), None, None),
        P(),
        P(),
        P(),
        P(),
        P(),
    )
    out_specs = P(("member", "fld"), "lev", "lat", None)
    return jax.shard_map(local, mesh=mesh, in_specs=in_specs, out_specs=out_specs, check_vma=False)
```

```python
import jax
import jax.numpy as jnp
from jax import lax
from jax.sharding import PartitionSpec as P

PRECISE = lax.Precision.HIGHEST
CHUNKS = 2


def wave_table(waves, nlon):
    step = next(d for d in range(min(nlon, 128), 0, -1) if nlon % d == 0)
    unit = 2.0 * jnp.pi / nlon
    low = (waves[:, None] * jnp.arange(step, dtype=jnp.int32)[None, :]) % nlon
    high = (waves[:, None] * (step * jnp.arange(nlon // step, dtype=jnp.int32))[None, :]) % nlon
    low = low.astype(jnp.float32) * unit
    high = high.astype(jnp.float32) * unit
    cl, sl = jnp.cos(low), jnp.sin(low)
    ch, sh = jnp.cos(high), jnp.sin(high)
    first = jnp.stack([ch, -sh], axis=0)
    second = jnp.stack([sh, ch], axis=0)
    pieces = [
        (first[:, :, h, None] * cl - second[:, :, h, None] * sl).astype(jnp.bfloat16)
        for h in range(nlon // step)
    ]
    return jnp.concatenate(pieces, axis=2)


def local(
    grid_state,
    lat_order,
    slot_wave,
    truncation,
    zonal_wind,
    zonal_rate,
    quad_weight,
    legendre,
    vert_modes,
    vert_project,
    mode_rates,
    thermal_into_spread_matrix,
    pressure_balance_matrix,
):
    levd, latd, nlon = grid_state.shape[1:]
    slots = legendre.shape[0]
    nmodes = slot_wave.shape[0]
    nlat = lat_order.shape[0]
    nlev = vert_modes.shape[0]
    nlats = lax.axis_size("lat")
    nlevs = lax.axis_size("lev")
    nfld = lax.axis_size("fld")
    lat_index = lax.axis_index("lat")
    lev_index = lax.axis_index("lev")
    fld_index = lax.axis_index("fld")
    owners = nlats * nlevs
    dests = owners * nfld
    per = -(-slots // nfld)
    spare = per * nfld - slots
    chunks = CHUNKS if per % CHUNKS == 0 else 1
    part = per // chunks

    waves = jnp.pad(slot_wave.reshape(owners, slots), ((0, 0), (0, spare)))
    waves = waves.reshape(dests, per)
    me = (lat_index * nlevs + lev_index) * nfld + fld_index
    my_waves = lax.dynamic_index_in_dim(waves, me, 0, keepdims=False)
    leg = jnp.pad(legendre, ((0, spare), (0, 0), (0, 0)))
    leg = lax.dynamic_slice_in_dim(leg, fld_index * per, per, 0)
    lats = jnp.arange(nlat, dtype=jnp.int32)
    hits = lat_order[:, None] == lats[None, :]
    leg = jnp.einsum(
        "skl,rl->skr", leg, hits.astype(jnp.bfloat16), preferred_element_type=jnp.float32
    ).astype(jnp.bfloat16)

    my_hits = lax.dynamic_slice_in_dim(hits, lat_index * latd, latd, 0)
    pick = lambda column: jnp.sum(jnp.where(my_hits, column[None, :], 0.0), axis=1)
    wind, rate, weight = pick(zonal_wind), pick(zonal_rate), pick(quad_weight)
    grid = grid_state[0]
    values = grid.astype(jnp.float32)
    flux = (values * (wind[None, :, None] + values)).astype(jnp.bfloat16)

    degree = jnp.arange(nmodes, dtype=jnp.int32)
    mode_hits = my_waves[:, None] == degree[None, :]
    limits = jnp.sum(jnp.where(mode_hits, truncation[None, :], 0), axis=1)
    n_int = my_waves[:, None] + degree[None, :]
    valid = n_int <= limits[:, None]
    n_deg = n_int.astype(jnp.float32)
    h = n_deg * (n_deg + 1.0) / (nmodes * (nmodes - 1))

    mixed = jnp.dot(vert_project, thermal_into_spread_matrix, precision=PRECISE)
    into = jnp.concatenate([vert_project, mixed], axis=1)
    pressed = jnp.dot(pressure_balance_matrix, vert_modes, precision=PRECISE)
    out_of = jnp.concatenate([vert_modes, -pressed], axis=0)

    table = wave_table(waves.reshape(-1), nlon).reshape(2, dests, per, nlon)
    table = jnp.transpose(table, (1, 0, 2, 3))
    dims = (((3,), (2,)), ((), ()))
    scale = nlon ** (-0.5)
    plain = lax.dot_general(table, grid, dims, preferred_element_type=jnp.float32) * scale
    moved = lax.dot_general(table, flux, dims, preferred_element_type=jnp.float32) * scale
    factor = waves.astype(jnp.float32)[:, :, None, None] * rate
    real = ((plain[:, 0] + factor * moved[:, 1]) * weight).astype(jnp.bfloat16)
    imag = ((plain[:, 1] - factor * moved[:, 0]) * weight).astype(jnp.bfloat16)

    returned, landed, sent = [], [], []
    for i in range(chunks):
        cut = slice(i * part, (i + 1) * part)
        fourier = jnp.stack([real[:, cut], imag[:, cut]], axis=1)
        if landed:
            fourier, landed[-1] = lax.optimization_barrier((fourier, landed[-1]))
        arrived = lax.all_to_all(
            fourier, ("lat", "lev", "fld"), split_axis=0, concat_axis=0, tiled=True
        )
        landed.append(arrived)
    for i in range(chunks):
        cut = slice(i * part, (i + 1) * part)
        arrived = landed[i]
        if sent:
            arrived, sent[-1] = lax.optimization_barrier((arrived, sent[-1]))
        arrived = arrived.reshape(nlats, nlevs, nfld, 2, part, levd, latd)
        arranged = jnp.transpose(arrived, (4, 3, 2, 1, 5, 0, 6)).reshape(part, 4 * nlev, nlat)
        mine = leg[cut]
        spec = jnp.einsum("sxr,skr->sxk", arranged, mine, preferred_element_type=jnp.float32)
        spec = spec.reshape(part, 2, 2, nlev, nmodes)
        hc = h[cut][:, None, None, :]
        vc = valid[cut][:, None, None, :]
        div = jnp.where(vc, spec[:, :, 0], 0.0)
        temp = jnp.where(vc, spec[:, :, 1], 0.0)
        source = jnp.concatenate([div, hc * temp], axis=2)
        projected = jnp.einsum("ij,scjk->scik", into, source, precision=lax.Precision.HIGH)
        projected = projected / (1.0 + hc * mode_rates[:, None])
        new = jnp.einsum("ij,scjk->scik", out_of, projected, precision=lax.Precision.HIGH)
        new = new.reshape(part, 2, 2, nlev, nmodes)
        new = jnp.stack([new[:, :, 0], temp + new[:, :, 1]], axis=2).astype(jnp.bfloat16)
        new = new.reshape(part, 4 * nlev, nmodes)
        back = jnp.einsum("sxk,skr->sxr", new, mine, preferred_element_type=jnp.float32)
        back = (back * nmodes ** (-0.5)).astype(jnp.bfloat16)
        back = back.reshape(part, 2, nfld, nlevs, levd, nlats, latd)
        outgoing = jnp.transpose(back, (5, 3, 2, 1, 0, 4, 6)).reshape(dests, 2, part, levd, latd)
        sent.append(outgoing)
    for outgoing in sent:
        if returned:
            outgoing, returned[-1] = lax.optimization_barrier((outgoing, returned[-1]))
        returned.append(
            lax.all_to_all(
                outgoing, ("lat", "lev", "fld"), split_axis=0, concat_axis=0, tiled=True
            )
        )
    leading = jnp.concatenate(returned, axis=2)
    dims = (((0, 1, 2), (0, 1, 2)), ((), ()))
    grid_out = lax.dot_general(leading, table, dims, preferred_element_type=jnp.float32)
    return (grid_out * nmodes ** (-0.5)).astype(jnp.bfloat16)[None]


def solution(mesh):
    in_specs = (
        P(("member", "fld"), "lev", "lat", None),
        P(),
        P(),
        P(),
        P(),
        P(),
        P(),
        P(("lat", "lev"), None, None),
        P(),
        P(),
        P(),
        P(),
        P(),
    )
    out_specs = P(("member", "fld"), "lev", "lat", None)
    return jax.shard_map(local, mesh=mesh, in_specs=in_specs, out_specs=out_specs, check_vma=False)
```

```python
import jax
import jax.numpy as jnp
from jax import lax
from jax.sharding import PartitionSpec as P

PRECISE = lax.Precision.HIGHEST
CHUNKS = 2


def wave_table(waves, nlon):
    step = next(d for d in range(min(nlon, 128), 0, -1) if nlon % d == 0)
    unit = 2.0 * jnp.pi / nlon
    low = (waves[:, None] * jnp.arange(step, dtype=jnp.int32)[None, :]) % nlon
    high = (waves[:, None] * (step * jnp.arange(nlon // step, dtype=jnp.int32))[None, :]) % nlon
    low = low.astype(jnp.float32) * unit
    high = high.astype(jnp.float32) * unit
    cl, sl = jnp.cos(low), jnp.sin(low)
    ch, sh = jnp.cos(high), jnp.sin(high)
    first = jnp.stack([ch, -sh], axis=0)
    second = jnp.stack([sh, ch], axis=0)
    pieces = [
        (first[:, :, h, None] * cl - second[:, :, h, None] * sl).astype(jnp.bfloat16)
        for h in range(nlon // step)
    ]
    return jnp.concatenate(pieces, axis=2)


def local(
    grid_state,
    lat_order,
    slot_wave,
    truncation,
    zonal_wind,
    zonal_rate,
    quad_weight,
    legendre,
    vert_modes,
    vert_project,
    mode_rates,
    thermal_into_spread_matrix,
    pressure_balance_matrix,
):
    levd, latd, nlon = grid_state.shape[1:]
    slots = legendre.shape[0]
    nmodes = slot_wave.shape[0]
    nlat = lat_order.shape[0]
    nlev = vert_modes.shape[0]
    nlats = lax.axis_size("lat")
    nlevs = lax.axis_size("lev")
    nfld = lax.axis_size("fld")
    lat_index = lax.axis_index("lat")
    lev_index = lax.axis_index("lev")
    fld_index = lax.axis_index("fld")
    owners = nlats * nlevs
    dests = owners * nfld
    per = -(-slots // nfld)
    spare = per * nfld - slots
    chunks = CHUNKS if per % CHUNKS == 0 else 1
    part = per // chunks

    waves = jnp.pad(slot_wave.reshape(owners, slots), ((0, 0), (0, spare)))
    waves = waves.reshape(dests, per)
    me = (lat_index * nlevs + lev_index) * nfld + fld_index
    my_waves = lax.dynamic_index_in_dim(waves, me, 0, keepdims=False)
    leg = jnp.pad(legendre, ((0, spare), (0, 0), (0, 0)))
    leg = lax.dynamic_slice_in_dim(leg, fld_index * per, per, 0)
    lats = jnp.arange(nlat, dtype=jnp.int32)
    hits = lat_order[:, None] == lats[None, :]
    leg = jnp.einsum(
        "skl,rl->skr", leg, hits.astype(jnp.bfloat16), preferred_element_type=jnp.float32
    ).astype(jnp.bfloat16)

    my_hits = lax.dynamic_slice_in_dim(hits, lat_index * latd, latd, 0)
    pick = lambda column: jnp.sum(jnp.where(my_hits, column[None, :], 0.0), axis=1)
    wind, rate, weight = pick(zonal_wind), pick(zonal_rate), pick(quad_weight)
    grid = grid_state[0]
    values = grid.astype(jnp.float32)
    flux = (values * (wind[None, :, None] + values)).astype(jnp.bfloat16)

    degree = jnp.arange(nmodes, dtype=jnp.int32)
    mode_hits = my_waves[:, None] == degree[None, :]
    limits = jnp.sum(jnp.where(mode_hits, truncation[None, :], 0), axis=1)
    n_int = my_waves[:, None] + degree[None, :]
    valid = n_int <= limits[:, None]
    n_deg = n_int.astype(jnp.float32)
    h = n_deg * (n_deg + 1.0) / (nmodes * (nmodes - 1))

    mixed = jnp.dot(vert_project, thermal_into_spread_matrix, precision=PRECISE)
    into = jnp.concatenate([vert_project, mixed], axis=1)
    pressed = jnp.dot(pressure_balance_matrix, vert_modes, precision=PRECISE)
    out_of = jnp.concatenate([vert_modes, -pressed], axis=0)

    table = wave_table(waves.reshape(-1), nlon).reshape(2, dests, per, nlon)
    table = jnp.transpose(table, (1, 0, 2, 3))
    dims = (((3,), (2,)), ((), ()))
    scale = nlon ** (-0.5)
    returned, landed, sent = [], [], []
    for i in range(chunks):
        cut = slice(i * part, (i + 1) * part)
        mine = table[:, :, cut]
        plain = lax.dot_general(mine, grid, dims, preferred_element_type=jnp.float32) * scale
        moved = lax.dot_general(mine, flux, dims, preferred_element_type=jnp.float32) * scale
        if landed:
            plain, moved, landed[-1] = lax.optimization_barrier((plain, moved, landed[-1]))
        factor = waves[:, cut].astype(jnp.float32)[:, :, None, None] * rate
        real = (plain[:, 0] + factor * moved[:, 1]) * weight
        imag = (plain[:, 1] - factor * moved[:, 0]) * weight
        fourier = jnp.stack([real, imag], axis=1).astype(jnp.bfloat16)
        arrived = lax.all_to_all(
            fourier, ("lat", "lev", "fld"), split_axis=0, concat_axis=0, tiled=True
        )
        landed.append(arrived)
    for i in range(chunks):
        cut = slice(i * part, (i + 1) * part)
        arrived = landed[i]
        if sent:
            arrived, sent[-1] = lax.optimization_barrier((arrived, sent[-1]))
        arrived = arrived.reshape(nlats, nlevs, nfld, 2, part, levd, latd)
        arranged = jnp.transpose(arrived, (4, 3, 2, 1, 5, 0, 6)).reshape(part, 4 * nlev, nlat)
        mine = leg[cut]
        spec = jnp.einsum("sxr,skr->sxk", arranged, mine, preferred_element_type=jnp.float32)
        spec = spec.reshape(part, 2, 2, nlev, nmodes)
        hc = h[cut][:, None, None, :]
        vc = valid[cut][:, None, None, :]
        div = jnp.where(vc, spec[:, :, 0], 0.0)
        temp = jnp.where(vc, spec[:, :, 1], 0.0)
        source = jnp.concatenate([div, hc * temp], axis=2)
        projected = jnp.einsum("ij,scjk->scik", into, source, precision=lax.Precision.HIGH)
        projected = projected / (1.0 + hc * mode_rates[:, None])
        new = jnp.einsum("ij,scjk->scik", out_of, projected, precision=lax.Precision.HIGH)
        new = new.reshape(part, 2, 2, nlev, nmodes)
        new = jnp.stack([new[:, :, 0], temp + new[:, :, 1]], axis=2).astype(jnp.bfloat16)
        new = new.reshape(part, 4 * nlev, nmodes)
        back = jnp.einsum("sxk,skr->sxr", new, mine, preferred_element_type=jnp.float32)
        back = (back * nmodes ** (-0.5)).astype(jnp.bfloat16)
        back = back.reshape(part, 2, nfld, nlevs, levd, nlats, latd)
        outgoing = jnp.transpose(back, (5, 3, 2, 1, 0, 4, 6)).reshape(dests, 2, part, levd, latd)
        sent.append(outgoing)
    for outgoing in sent:
        if returned:
            outgoing, returned[-1] = lax.optimization_barrier((outgoing, returned[-1]))
        returned.append(
            lax.all_to_all(
                outgoing, ("lat", "lev", "fld"), split_axis=0, concat_axis=0, tiled=True
            )
        )
    leading = jnp.concatenate(returned, axis=2)
    dims = (((0, 1, 2), (0, 1, 2)), ((), ()))
    grid_out = lax.dot_general(leading, table, dims, preferred_element_type=jnp.float32)
    return (grid_out * nmodes ** (-0.5)).astype(jnp.bfloat16)[None]


def solution(mesh):
    in_specs = (
        P(("member", "fld"), "lev", "lat", None),
        P(),
        P(),
        P(),
        P(),
        P(),
        P(),
        P(("lat", "lev"), None, None),
        P(),
        P(),
        P(),
        P(),
        P(),
    )
    out_specs = P(("member", "fld"), "lev", "lat", None)
    return jax.shard_map(local, mesh=mesh, in_specs=in_specs, out_specs=out_specs, check_vma=False)
```
